256 devices in a mesh: section: 8 (over z), ctx: 32 (over x, y, core).
Axes of the slice: x: 4, y: 4, z: 8, core: 2. Of those that a mesh axis runs over, the one named last changes fastest.
Arguments:
- queries: bfloat16 [8, 4096, 4096], P('section', 'ctx'), may hold values from -130 to 130
- keys_new: bfloat16 [8, 4096, 1024], P('section', 'ctx'), may hold values from -6 to 6
- values_new: bfloat16 [8, 4096, 1024], P('section', 'ctx'), may hold values from -6 to 6
- stretch_cache: bfloat16 [8, 2048, 2048], P('section'), may hold values from -6 to 6
- hadamard_signs: int32 [8, 2, 128], P('section'), may hold values from -1 to 1, as said below
- stretch_docs: int32 [32], replicated, may hold values from 0 to 7, never falling along the last dimension, each value on 1 to 17 neighbouring positions
Outputs:
- handed: bfloat16 [8, 4096, 4096], P('section', 'ctx')
The draws below stay inside these ranges and needn't reach their ends.
Inputs may be any that keep to these rules, and one draw needn't show every extreme that they name: `hadamard_signs`: each entry is -1 or 1. `stretch_docs`: never falling along the stretches; each document covers 1 to 17 stretches in a row.
All inputs are finite; a program needn't handle non-finite values.
Results may differ from the reference program's by a relative error of at most 0.0099.
Values may be sent and summed in bfloat16 or wider, within the bound.
No kernel may reach another device: no remote copies, remote signals or barrier semaphores. Data moves between devices by JAX's collectives and lax.ppermute only.
A program may use at most 128 MiB of HBM per device.

```python
import math
import jax
import jax.numpy as jnp
import numpy as np
from jax import lax

QH = 32
KVH = 8
HD = 128
ROWS = 128
CACHE = 256
SECTIONS = 8
STRETCHES = 32
TOKENS = 4096
SPAN = 17
DOCS = 8
N_CTX = 32


def draw_queries(key, part):
    first_key = jax.random.fold_in(jax.random.fold_in(key, 11), 0)
    shape_all = (SECTIONS, TOKENS, QH * HD)
    base = jnp.clip(2.5 * jax.random.normal(first_key, shape_all, jnp.float32), -10.0, 10.0)
    return base.astype(jnp.bfloat16)


def draw_hadamard_signs(key, part):
    picks = jax.random.randint(jax.random.fold_in(key, 23), (SECTIONS, 2, HD), 0, 2)
    return (2 * picks - 1).astype(jnp.int32)


def shard_levels(own_key, extent, cuts, smallest, largest):
    def one(axis_at, shards_of):
        heights = jax.random.uniform(jax.random.fold_in(jax.random.fold_in(own_key, 6), axis_at), (shards_of,), jnp.float32, smallest / len(cuts), largest / len(cuts))
        return jnp.repeat(jnp.exp(heights), extent[axis_at] // shards_of).reshape((-1,) + (1,) * (len(extent) - axis_at - 1))

    gain = one(*cuts[0])
    for cut in cuts[1:]:
        gain = gain * one(*cut)
    return gain


def length_profile(number_of, total, reach, slope):
    loads = [(1 << 20) // math.isqrt(rank ** slope) + 1 for rank in range(2, number_of + 1)]
    surplus, holding = total - reach - (number_of - 1), [1] * (number_of - 1)
    while surplus > 0:
        movable = [i for i in range(number_of - 1) if holding[i] < reach]
        whole, left = sum([loads[i] for i in movable]), surplus
        for i in movable:
            extra = min(reach - holding[i], max(1, left * loads[i] // whole), surplus)
            holding[i] = holding[i] + extra
            surplus = surplus - extra
    return np.array([reach] + holding)


def uneven(key, number_of, total, most, slope):
    if number_of == 2:
        one = jax.random.randint(key, (), max(1, total - most), min(most, total - 1) + 1)
        return jnp.stack([one, total - one])
    tallies = jnp.asarray(length_profile(number_of, total, most, slope), jnp.int32)
    pairs = (number_of - 1) // 2
    donor, sink = tallies[1:1 + 2 * pairs:2], tallies[2:2 + 2 * pairs:2]
    room = jnp.minimum(donor - 1, most - sink)
    passed = jax.random.randint(jax.random.fold_in(key, 1), (pairs,), 0, 1 << 20) % (room + 1)
    tallies = tallies.at[1:1 + 2 * pairs:2].set(donor - passed).at[2:2 + 2 * pairs:2].set(sink + passed)
    return tallies[jax.random.permutation(jax.random.fold_in(key, 2), number_of)]


def centred(rng, extent, width, reach, cuts=(), kind=jnp.bfloat16):
    values = width * jax.random.normal(rng, extent, jnp.float32)
    if cuts:
        values = values * shard_levels(rng, extent, cuts, -0.22, 0.18)
    return jnp.clip(values, -reach, reach).astype(kind)


def setup_inputs(seed: int = 0) -> dict:
    arg_keys = jax.random.split(jax.random.key(seed), 7)
    return {
        "queries": draw_queries(jax.random.fold_in(arg_keys[6], 71), 0),
        "keys_new": centred(arg_keys[1], (SECTIONS, TOKENS, KVH * HD), 1.0, 6.0, ((0, 8), (1, 32))),
        "values_new": centred(arg_keys[2], (SECTIONS, TOKENS, KVH * HD), 1.0, 6.0, ((0, 8), (1, 32))),
        "stretch_cache": centred(arg_keys[3], (SECTIONS, DOCS * CACHE, 2 * KVH * HD), 1.0, 6.0, ((0, 8),)),
        "hadamard_signs": draw_hadamard_signs(jax.random.fold_in(arg_keys[6], 71), 0),
        "stretch_docs": jnp.searchsorted(jnp.cumsum(uneven(arg_keys[5], DOCS, STRETCHES, SPAN, 0)), jnp.arange(STRETCHES), side="right").astype(jnp.int32),
    }


def hadamard(length):
    numbers = np.arange(length)
    common = numbers[:, None] & numbers[None, :]
    parity = np.zeros((length, length), np.int64)
    for bit_place in range(max(int(length).bit_length(), 1)):
        parity = parity ^ ((common >> bit_place) & 1)
    return 1.0 - 2.0 * parity


def rotate(source, sign_row, rotation):
    row_count = source.shape[0]
    head_size = rotation.shape[0]
    shaped = (source.reshape(row_count, -1, head_size) * sign_row.astype(source.dtype)).reshape(-1, head_size)
    turned = jnp.dot(shaped, rotation, preferred_element_type=jnp.float32) * (head_size ** -0.5)
    return turned.reshape(row_count, -1).astype(jnp.bfloat16)


def reference(queries, keys_new, values_new, stretch_cache, hadamard_signs, stretch_docs):
    rotation = jnp.asarray(hadamard(HD), dtype=jnp.bfloat16)
    inverse = jnp.asarray(hadamard(HD), dtype=jnp.float32)
    groups = QH // KVH

    def one_section(section_args):
        section_query, section_keys, section_values, section_cache, section_signs = section_args
        fronts = jnp.concatenate([rotate(section_keys, section_signs[0], rotation), rotate(section_values, section_signs[1], rotation)], axis=1)

        def one_stretch(stretch_index):
            query_rows = lax.dynamic_slice_in_dim(section_query, stretch_index * ROWS, ROWS, 0)
            query_turned = rotate(query_rows, section_signs[0], rotation).reshape(ROWS, KVH, groups, HD)
            doc_mine = stretch_docs[stretch_index]
            own_cache = lax.dynamic_slice_in_dim(section_cache, (doc_mine * CACHE).astype(jnp.int32), CACHE, 0)
            keyset = jnp.concatenate([own_cache, fronts], axis=0)
            key_part = keyset[:, :KVH * HD].reshape(-1, KVH, HD)
            value_part = keyset[:, KVH * HD:].reshape(-1, KVH, HD)
            scores = jnp.einsum("rkgd,nkd->rkgn", query_turned.astype(jnp.float32), key_part.astype(jnp.float32)) * (HD ** -0.5)
            position = jnp.arange(TOKENS, dtype=jnp.int32)
            key_stretch = position // ROWS
            key_row = position % ROWS
            query_row = jnp.arange(ROWS, dtype=jnp.int32)
            doc_keys = stretch_docs[key_stretch]
            same_stretch = (key_stretch[None, :] == stretch_index) & (key_row[None, :] <= query_row[:, None])
            earlier = (key_stretch[None, :] < stretch_index) & (doc_keys[None, :] == doc_mine)
            allowed = jnp.concatenate([jnp.ones((ROWS, CACHE), dtype=bool), same_stretch | earlier], axis=1)
            scores = jnp.where(allowed[:, None, None, :], scores, -jnp.inf)
            row_max = scores.max(-1, keepdims=True)
            exponent = jnp.exp(scores - row_max)
            row_sum = exponent.sum(-1)
            weights = exponent.astype(jnp.bfloat16)
            averaged = jnp.einsum("rkgn,nkd->rkgd", weights.astype(jnp.float32), value_part.astype(jnp.float32)) / row_sum[..., None]
            restored = jnp.dot(averaged.reshape(-1, HD), inverse, precision=lax.Precision.HIGHEST)
            restored = restored * (HD ** -0.5) * section_signs[1].astype(jnp.float32)
            return restored.reshape(ROWS, QH * HD).astype(jnp.bfloat16)

        return lax.map(one_stretch, jnp.arange(N_CTX, dtype=jnp.int32)).reshape(TOKENS, QH * HD)

    heads_out = lax.map(one_section, (queries, keys_new, values_new, stretch_cache, hadamard_signs))
    return jnp.roll(heads_out, 1, axis=0)
```

```python
import functools

import jax
import jax.numpy as jnp
import numpy as np
from jax import lax
from jax.experimental import pallas as pl
from jax.experimental.pallas import tpu as pltpu
from jax.sharding import Mesh
from jax.sharding import PartitionSpec as P

HD = 128
ROWS = 128
KVH = 8
GROUP = 4
CACHE = 256
N_CTX = 32
DOCS = 8
QW = GROUP * HD
MIB = 1024 * 1024

CTX = ("x", "h", "l", "c")


def hadamard(length):
    numbers = np.arange(length)
    common = numbers[:, None] & numbers[None, :]
    parity = np.zeros((length, length), np.int64)
    for bit_place in range(max(int(length).bit_length(), 1)):
        parity = parity ^ common >> bit_place & 1
    return 1.0 - 2.0 * parity


def dot(a, b, dims):
    return lax.dot_general(a, b, (dims, ((), ())), preferred_element_type=jnp.float32)


def pack_q_kernel(q_ref, o_ref):
    for i in range(o_ref.shape[0]):
        o_ref[i] = q_ref[:, i * QW : (i + 1) * QW]


def pack_q(queries):
    steps = 2
    per = KVH // steps
    return pl.pallas_call(
        pack_q_kernel,
        grid=(steps,),
        in_specs=[pl.BlockSpec((ROWS, per * QW), lambda i: (0, i))],
        out_specs=pl.BlockSpec((per, ROWS, QW), lambda i: (i, 0, 0)),
        out_shape=jax.ShapeDtypeStruct((KVH, ROWS, QW), jnp.bfloat16),
        cost_estimate=pl.CostEstimate(flops=0, bytes_accessed=4 * KVH * ROWS * QW, transcendentals=0),
        compiler_params=pltpu.CompilerParams(vmem_limit_bytes=60 * MIB),
        name="pack_q",
    )(queries)


def pack_kv_kernel(k_ref, v_ref, o_ref):
    for i in range(o_ref.shape[0]):
        for low in range(2):
            lanes = slice((2 * i + low) * HD, (2 * i + low + 1) * HD)
            keys = k_ref[:, lanes]
            values = v_ref[:, lanes].T
            for high in range(2):
                o_ref[i, high, low, 0] = keys
                o_ref[i, high, low, 1] = values


def pack_kv(keys, values):
    steps = 2
    per = 4 // steps
    return pl.pallas_call(
        pack_kv_kernel,
        grid=(steps,),
        in_specs=[pl.BlockSpec((ROWS, 2 * per * HD), lambda i: (0, i))] * 2,
        out_specs=pl.BlockSpec((per, 2, 2, 2, ROWS, HD), lambda i: (i, 0, 0, 0, 0, 0)),
        out_shape=jax.ShapeDtypeStruct((4, 2, 2, 2, ROWS, HD), jnp.bfloat16),
        cost_estimate=pl.CostEstimate(flops=0, bytes_accessed=6 * KVH * ROWS * QW // 2, transcendentals=0),
        compiler_params=pltpu.CompilerParams(vmem_limit_bytes=60 * MIB),
        name="pack_kv",
    )(keys, values)


def turn_kernel(place, ck_ref, cv_ref, had_ref, sk_ref, sv_ref, k_out, v_out):
    had = had_ref[...]
    for d in range(k_out.shape[0]):
        rows = slice(d * CACHE, (d + 1) * CACHE)
        turned = dot(ck_ref[0, rows, :], had, ((1,), (0,))) * np.float32(HD**-0.5)
        k_out[d] = (turned * sk_ref[...]).astype(jnp.bfloat16)
        turned = dot(had, cv_ref[0, rows, :], ((1,), (1,))) * np.float32(HD**-0.5)
        v_out[d] = (turned * sv_ref[...]).astype(jnp.bfloat16)


def turn_cache(place, cache, had, sign_k, sign_v):
    whole = pl.BlockSpec(memory_space=pltpu.VMEM)
    rows = DOCS * CACHE
    return pl.pallas_call(
        turn_kernel,
        grid_spec=pltpu.PrefetchScalarGridSpec(
            num_scalar_prefetch=1,
            grid=(1,),
            in_specs=[
                pl.BlockSpec((1, rows, HD), lambda i, at: (0, 0, at[0] * 2 + at[2])),
                pl.BlockSpec((1, rows, HD), lambda i, at: (0, 0, KVH + at[0] * 2 + at[2])),
                pl.BlockSpec((HD, HD), lambda i, at: (0, 0)),
                pl.BlockSpec((1, HD), lambda i, at: (0, 0)),
                pl.BlockSpec((HD, 1), lambda i, at: (0, 0)),
            ],
            out_specs=[whole, whole],
        ),
        out_shape=[
            jax.ShapeDtypeStruct((DOCS, CACHE, HD), jnp.bfloat16),
            jax.ShapeDtypeStruct((DOCS, HD, CACHE), jnp.bfloat16),
        ],
        cost_estimate=pl.CostEstimate(flops=8 * DOCS * CACHE * HD * HD, bytes_accessed=8 * DOCS * CACHE * HD, transcendentals=0),
        compiler_params=pltpu.CompilerParams(vmem_limit_bytes=56 * MIB),
        name="turn_cache",
    )(place, cache, cache, had, sign_k, sign_v)


PAIR = 2 * ROWS
MOST_PAIRS = 8
SIZES = (4, 2, 1)
BOTH = range(2)


def attend_kernel(
    begin,
    place,
    docs,
    firsts,
    q_ref,
    k_ref,
    v_ref,
    ck_hbm,
    cv_hbm,
    o_ref,
    ck_ref,
    cv_ref,
    sem,
    qt,
    scores,
    acc,
    tops,
    sums,
):
    src_x = lax.rem(place[0] + begin + 2 * pl.program_id(0), 4)
    scale = np.float32(HD**-0.5 * np.log2(np.e))
    mes = [src_x * 8 + place[1] * 4 + n * 2 + place[3] for n in BOTH]
    first = [firsts[me] for me in mes]
    doc = [docs[me] for me in mes]
    before = [mes[n] - first[n] for n in BOTH]
    pairs = [before[n] // 2 for n in BOTH]
    beside = [jnp.maximum(me - 1, 0) for me in mes]

    k_copy = pltpu.make_async_copy(ck_hbm, ck_ref, sem.at[0])
    v_copy = pltpu.make_async_copy(cv_hbm, cv_ref, sem.at[1])

    @pl.when(pl.program_id(0) == 0)
    def _():
        k_copy.start()
        v_copy.start()

    def fold(s):
        return s.reshape(-1, 8, QW)

    def regions(n, work):
        big = SIZES[0]

        def body(i, carry):
            work(n, i * big, big)
            return carry

        lax.fori_loop(0, pairs[n] // big, body, 0)
        done = pairs[n] // big * big
        for size in SIZES[1:]:
            need = (pairs[n] & size) != 0

            @pl.when(need)
            def _(done=done, size=size):
                work(n, done, size)

            done = done + jnp.where(need, size, 0)

    key_at = lax.broadcasted_iota(jnp.int32, (PAIR, QW), 0)
    query_at = lax.broadcasted_iota(jnp.int32, (PAIR, QW), 1) % ROWS + ROWS
    causal = key_at <= query_at
    for n in BOTH:
        for g in range(GROUP):
            lanes = slice(g * HD, (g + 1) * HD)
            qt[n, :, lanes] = q_ref[n, :, lanes].T
    for n in BOTH:
        keys = jnp.concatenate([k_ref[beside[n]], k_ref[mes[n]]], axis=0)
        lowest = jnp.where(before[n] % 2 == 1, 0, ROWS)
        s_own = dot(keys, qt[n], ((1,), (0,)))
        s_own = jnp.where(causal & (key_at >= lowest), s_own, -jnp.inf)
        scores[n, 1] = s_own
        tops[n] = jnp.max(fold(s_own), axis=0)

    def look(n, begin_at, count):
        best = tops[n]
        for j in range(count):
            i = begin_at + j
            keys = k_ref[pl.ds(first[n] + 2 * i, 2)].reshape(PAIR, HD)
            s = dot(keys, qt[n], ((1,), (0,)))
            scores[n, 2 + i] = s
            best = jnp.maximum(best, jnp.max(fold(s), axis=0))
        tops[n] = best

    for n in BOTH:
        regions(n, look)

    @pl.when(pl.program_id(0) == 0)
    def _():
        k_copy.wait()
        v_copy.wait()

    for n in BOTH:
        s_cache = dot(ck_ref[doc[n]], qt[n], ((1,), (0,)))
        scores[n, 0] = s_cache
        top = jnp.maximum(tops[n], jnp.max(fold(s_cache), axis=0))
        tops[n] = jnp.broadcast_to(jnp.max(top, axis=0, keepdims=True) * scale, (8, QW))

    def weigh(n, i, top):
        p = jnp.exp2(scores[n, i] * scale - top)
        return p.astype(jnp.bfloat16), jnp.sum(fold(p), axis=0)

    for n in BOTH:
        top = tops[n, 0:1]
        p_cache, l_cache = weigh(n, 0, top)
        p_own, l_own = weigh(n, 1, top)
        values = jnp.concatenate([v_ref[beside[n]], v_ref[mes[n]]], axis=1)
        acc[n] = dot(cv_ref[doc[n]], p_cache, ((1,), (0,))) + dot(values, p_own, ((1,), (0,)))
        sums[n] = l_cache + l_own

    def add(n, begin_at, count):
        top = tops[n, 0:1]
        total = sums[n]
        out = acc[n]
        for j in range(count):
            i = begin_at + j
            p, l = weigh(n, 2 + i, top)
            at = first[n] + 2 * i
            values = jnp.concatenate([v_ref[at], v_ref[at + 1]], axis=1)
            out = out + dot(values, p, ((1,), (0,)))
            total = total + l
        sums[n] = total
        acc[n] = out

    for n in BOTH:
        regions(n, add)

    for n in BOTH:
        out = acc[n] * (1.0 / jnp.sum(sums[n], axis=0, keepdims=True))
        for g in range(GROUP):
            lanes = slice(g * HD, (g + 1) * HD)
            o_ref[n, :, lanes] = out[:, lanes].astype(jnp.bfloat16).T


def attend(begin, steps, place, docs, firsts, queries, keys, values, cache_k, cache_v):
    def q_at(i, place, docs, firsts):
        return (lax.rem(place[0] + begin + 2 * i, 4), 0, 0)

    whole = pl.BlockSpec(memory_space=pltpu.VMEM)
    there = pl.BlockSpec(memory_space=pl.ANY)
    return pl.pallas_call(
        functools.partial(attend_kernel, begin),
        grid_spec=pltpu.PrefetchScalarGridSpec(
            num_scalar_prefetch=3,
            grid=(steps,),
            in_specs=[pl.BlockSpec((2, ROWS, QW), q_at), whole, whole, there, there],
            out_specs=pl.BlockSpec((2, ROWS, QW), lambda i, place, docs, firsts: (i, 0, 0)),
            scratch_shapes=[
                pltpu.VMEM((DOCS, CACHE, HD), jnp.bfloat16),
                pltpu.VMEM((DOCS, HD, CACHE), jnp.bfloat16),
                pltpu.SemaphoreType.DMA((2,)),
                pltpu.VMEM((2, HD, QW), jnp.bfloat16),
                pltpu.VMEM((2, 2 + MOST_PAIRS, PAIR, QW), jnp.float32),
                pltpu.VMEM((2, HD, QW), jnp.float32),
                pltpu.VMEM((2, 8, QW), jnp.float32),
                pltpu.VMEM((2, 8, QW), jnp.float32),
            ],
        ),
        out_shape=jax.ShapeDtypeStruct((2 * steps, ROWS, QW), jnp.bfloat16),
        compiler_params=pltpu.CompilerParams(vmem_limit_bytes=20 * MIB),
        cost_estimate=pl.CostEstimate(flops=steps * 48 * PAIR * QW * HD, bytes_accessed=steps * 4 * ROWS * QW, transcendentals=steps * 12 * PAIR * QW),
        name="attend",
    )(place, docs, firsts, queries, keys, values, cache_k, cache_v)


def join_kernel(offsets, place, *refs):
    pieces, out, sem = refs[: len(offsets)], refs[-2], refs[-1]
    copies = []
    for i, (dx, dl) in enumerate(offsets):
        head = lax.rem(place[0] + 4 - dx, 4) * 2 + lax.rem(place[2] + dl, 2)
        lanes = pl.ds(pl.multiple_of(head * QW, QW), QW)
        copies.append(pltpu.make_async_copy(pieces[i].at[0], out.at[:, lanes], sem.at[i]))
    for copy in copies:
        copy.start()
    for copy in copies:
        copy.wait()


def join(place, offsets, pieces, base):
    whole = pl.BlockSpec(memory_space=pltpu.VMEM)
    there = pl.BlockSpec(memory_space=pl.ANY)
    known = [] if base is None else [base]
    return pl.pallas_call(
        functools.partial(join_kernel, offsets),
        grid_spec=pltpu.PrefetchScalarGridSpec(
            num_scalar_prefetch=1,
            grid=(1,),
            in_specs=[whole] * len(pieces) + [there] * len(known),
            out_specs=there,
            scratch_shapes=[pltpu.SemaphoreType.DMA((len(pieces),))],
        ),
        out_shape=jax.ShapeDtypeStruct((ROWS, KVH * QW), jnp.bfloat16),
        input_output_aliases={} if base is None else {1 + len(pieces): 0},
        compiler_params=pltpu.CompilerParams(vmem_limit_bytes=4 * MIB),
        name="join",
    )(place, *pieces, *known)


def out_route(sections, dx, dl):
    route = []
    for z in range(sections):
        for x in range(4):
            for l in range(2):
                target = ((z + 1) % sections, (x + dx) % 4, l ^ dl)
                route.append(((z * 4 + x) * 2 + l, (target[0] * 4 + target[1]) * 2 + target[2]))
    return route


def per_device(queries, keys_new, values_new, stretch_cache, hadamard_signs, stretch_docs):
    place = jnp.stack([lax.axis_index(name) for name in CTX]).astype(jnp.int32)
    sections = lax.axis_size("section")
    had = jnp.asarray(hadamard(HD), dtype=jnp.bfloat16)
    signs = hadamard_signs[0].astype(jnp.float32)
    kv = pack_kv(keys_new[0], values_new[0])
    q = pack_q(queries[0])
    mine = lax.all_to_all(kv.reshape(N_CTX, ROWS, HD), CTX, 0, 0, tiled=True)
    cache_k, cache_v = turn_cache(place, stretch_cache, had, signs[0:1], signs[1].reshape(HD, 1))
    earlier = stretch_docs[None, :] < stretch_docs[:, None]
    firsts = jnp.sum(earlier, axis=1, dtype=jnp.int32)
    mine, q, cache_k, cache_v = lax.optimization_barrier((mine, q, cache_k, cache_v))
    other = lax.ppermute(mine, "c", [(0, 1), (1, 0)])
    q = lax.all_to_all(q, ("x", "l"), 0, 0, tiled=True)
    keys = jnp.where(place[3] == 0, mine, other)
    values = jnp.where(place[3] == 0, other, mine)
    result = None
    for begin in range(2):
        out = attend(begin, 2, place, stretch_docs, firsts, q, keys, values, cache_k, cache_v)
        offsets = [(begin + 2 * i, dl) for i in range(2) for dl in range(2)]
        pieces = []
        for i, (dx, dl) in enumerate(offsets):
            row = i // 2 * 2 + (place[2] + dl) % 2
            piece = lax.dynamic_slice_in_dim(out, row, 1, 0)
            pieces.append(lax.ppermute(piece, ("section", "x", "l"), out_route(sections, dx, dl)))
        result = join(place, offsets, pieces, result)
    return result[None]


def solution(mesh):
    sections = mesh.shape["section"]
    split = Mesh(mesh.devices.reshape(sections, 4, 2, 2, 2), ("section",) + CTX)
    rows = P("section", CTX, None)
    in_specs = (rows, rows, rows, P("section", None, None), P("section", None, None), P())
    return jax.shard_map(
        per_device, mesh=split, in_specs=in_specs, out_specs=rows, check_vma=False
    )
```

```python
import functools

import jax
import jax.numpy as jnp
import numpy as np
from jax import lax
from jax.experimental import pallas as pl
from jax.experimental.pallas import tpu as pltpu
from jax.sharding import Mesh
from jax.sharding import PartitionSpec as P

HD = 128
ROWS = 128
KVH = 8
GROUP = 4
CACHE = 256
N_CTX = 32
DOCS = 8
QW = GROUP * HD
MIB = 1024 * 1024
EARLY = (2, 1)
LATE = (3,)
GROUPS = ((0,), (2,), (1, 3))

CTX = ("x", "h", "l", "c")


def hadamard(length):
    numbers = np.arange(length)
    common = numbers[:, None] & numbers[None, :]
    parity = np.zeros((length, length), np.int64)
    for bit_place in range(max(int(length).bit_length(), 1)):
        parity = parity ^ common >> bit_place & 1
    return 1.0 - 2.0 * parity


def dot(a, b, dims):
    return lax.dot_general(a, b, (dims, ((), ())), preferred_element_type=jnp.float32)


def offsets():
    return [(dx, dl) for dx in range(4) for dl in range(2)]


def pack_q_kernel(place, q_ref, *outs):
    for (dx, dl), out in zip(offsets(), outs):
        head = lax.rem(place[0] + 4 - dx, 4) * 2 + lax.rem(place[2] + dl, 2)
        q = q_ref[:, pl.ds(pl.multiple_of(head * QW, QW), QW)]
        for g in range(GROUP):
            lanes = slice(g * HD, (g + 1) * HD)
            out[:, lanes] = q[:, lanes].T


def pack_q(place, queries):
    whole = pl.BlockSpec((ROWS, QW), lambda i, place: (0, 0))
    return pl.pallas_call(
        pack_q_kernel,
        grid_spec=pltpu.PrefetchScalarGridSpec(
            num_scalar_prefetch=1,
            grid=(1,),
            in_specs=[pl.BlockSpec((ROWS, KVH * QW), lambda i, place: (0, 0))],
            out_specs=[whole] * KVH,
        ),
        out_shape=[jax.ShapeDtypeStruct((ROWS, QW), jnp.bfloat16)] * KVH,
        cost_estimate=pl.CostEstimate(flops=0, bytes_accessed=4 * KVH * ROWS * QW, transcendentals=0),
        compiler_params=pltpu.CompilerParams(vmem_limit_bytes=60 * MIB),
        name="pack_q",
    )(place, queries)


def pack_kv_kernel(k_ref, v_ref, o_ref):
    for i in range(o_ref.shape[0]):
        for low in range(2):
            lanes = slice((2 * i + low) * HD, (2 * i + low + 1) * HD)
            keys = k_ref[:, lanes]
            values = v_ref[:, lanes].T
            for high in range(2):
                o_ref[i, high, low, 0] = keys
                o_ref[i, high, low, 1] = values


def pack_kv(keys, values):
    steps = 2
    per = 4 // steps
    return pl.pallas_call(
        pack_kv_kernel,
        grid=(steps,),
        in_specs=[pl.BlockSpec((ROWS, 2 * per * HD), lambda i: (0, i))] * 2,
        out_specs=pl.BlockSpec((per, 2, 2, 2, ROWS, HD), lambda i: (i, 0, 0, 0, 0, 0)),
        out_shape=jax.ShapeDtypeStruct((4, 2, 2, 2, ROWS, HD), jnp.bfloat16),
        cost_estimate=pl.CostEstimate(flops=0, bytes_accessed=6 * KVH * ROWS * QW // 2, transcendentals=0),
        compiler_params=pltpu.CompilerParams(vmem_limit_bytes=60 * MIB),
        name="pack_kv",
    )(keys, values)


def turn_kernel(place, ck_ref, cv_ref, had_ref, out):
    had = had_ref[...]
    for d in range(DOCS):
        rows = slice(d * CACHE, (d + 1) * CACHE)
        turned = dot(ck_ref[0, rows, :], had, ((1,), (0,))) * np.float32(HD**-0.5)
        out[d, 0] = turned.astype(jnp.bfloat16)
        turned = dot(had, cv_ref[0, rows, :], ((1,), (1,))) * np.float32(HD**-0.5)
        turned = turned.astype(jnp.bfloat16)
        for half in range(CACHE // HD):
            lanes = slice(half * HD, (half + 1) * HD)
            out[d, 1, lanes, :] = turned[:, lanes]


def turn_cache(place, cache, had):
    rows = DOCS * CACHE
    return pl.pallas_call(
        turn_kernel,
        grid_spec=pltpu.PrefetchScalarGridSpec(
            num_scalar_prefetch=1,
            grid=(1,),
            in_specs=[
                pl.BlockSpec((1, rows, HD), lambda i, at: (0, 0, at[0] * 2 + at[2])),
                pl.BlockSpec((1, rows, HD), lambda i, at: (0, 0, KVH + at[0] * 2 + at[2])),
                pl.BlockSpec((HD, HD), lambda i, at: (0, 0)),
            ],
            out_specs=pl.BlockSpec(memory_space=pltpu.VMEM),
        ),
        out_shape=jax.ShapeDtypeStruct((DOCS, 2, CACHE, HD), jnp.bfloat16),
        cost_estimate=pl.CostEstimate(
            flops=8 * DOCS * CACHE * HD * HD, bytes_accessed=8 * DOCS * CACHE * HD, transcendentals=0
        ),
        compiler_params=pltpu.CompilerParams(vmem_limit_bytes=56 * MIB),
        name="turn_cache",
    )(place, cache, cache, had)


PAIR = 2 * ROWS
MOST_PAIRS = 8
SIZES = (4, 2, 1)
BOTH = range(2)


def attend_kernel(
    dx,
    place,
    docs,
    firsts,
    q0_ref,
    q1_ref,
    k_ref,
    v_ref,
    cache_ref,
    o0_ref,
    o1_ref,
    scores,
    acc,
    tops,
    sums,
):
    q_refs, o_refs = (q0_ref, q1_ref), (o0_ref, o1_ref)
    src_x = lax.rem(place[0] + dx, 4)
    scale = np.float32(HD**-0.5 * np.log2(np.e))
    mes = [src_x * 8 + place[1] * 4 + lax.rem(place[2] + n, 2) * 2 + place[3] for n in BOTH]
    first = [firsts[me] for me in mes]
    doc = [docs[me] for me in mes]
    before = [mes[n] - first[n] for n in BOTH]
    pairs = [before[n] // 2 for n in BOTH]
    beside = [jnp.maximum(me - 1, 0) for me in mes]

    def fold(s):
        return s.reshape(-1, 8, QW)

    def regions(n, work):
        big = SIZES[0]

        def body(i, carry):
            work(n, i * big, big)
            return carry

        lax.fori_loop(0, pairs[n] // big, body, 0)
        done = pairs[n] // big * big
        for size in SIZES[1:]:
            need = (pairs[n] & size) != 0

            @pl.when(need)
            def _(done=done, size=size):
                work(n, done, size)

            done = done + jnp.where(need, size, 0)

    key_at = lax.broadcasted_iota(jnp.int32, (PAIR, QW), 0)
    query_at = lax.broadcasted_iota(jnp.int32, (PAIR, QW), 1) % ROWS + ROWS
    causal = key_at <= query_at
    for n in BOTH:
        keys = jnp.concatenate([k_ref[beside[n]], k_ref[mes[n]]], axis=0)
        lowest = jnp.where(before[n] % 2 == 1, 0, ROWS)
        s_own = dot(keys, q_refs[n][...], ((1,), (0,)))
        s_own = jnp.where(causal & (key_at >= lowest), s_own, -jnp.inf)
        scores[n, 1] = s_own
        tops[n] = jnp.max(fold(s_own), axis=0)

    def look(n, begin_at, count):
        best = tops[n]
        for j in range(count):
            i = begin_at + j
            keys = k_ref[pl.ds(first[n] + 2 * i, 2)].reshape(PAIR, HD)
            s = dot(keys, q_refs[n][...], ((1,), (0,)))
            scores[n, 2 + i] = s
            best = jnp.maximum(best, jnp.max(fold(s), axis=0))
        tops[n] = best

    for n in BOTH:
        regions(n, look)

    for n in BOTH:
        s_cache = dot(cache_ref[doc[n], 0], q_refs[n][...], ((1,), (0,)))
        scores[n, 0] = s_cache
        top = jnp.maximum(tops[n], jnp.max(fold(s_cache), axis=0))
        tops[n] = jnp.broadcast_to(jnp.max(top, axis=0, keepdims=True) * scale, (8, QW))

    def weigh(n, i, top):
        p = jnp.exp2(scores[n, i] * scale - top)
        return p.astype(jnp.bfloat16), jnp.sum(fold(p), axis=0)

    for n in BOTH:
        top = tops[n, 0:1]
        p_cache, l_cache = weigh(n, 0, top)
        p_own, l_own = weigh(n, 1, top)
        values = jnp.concatenate([v_ref[beside[n]], v_ref[mes[n]]], axis=1)
        cached = jnp.concatenate(
            [cache_ref[doc[n], 1, :HD], cache_ref[doc[n], 1, HD:]], axis=1
        )
        acc[n] = dot(cached, p_cache, ((1,), (0,))) + dot(values, p_own, ((1,), (0,)))
        sums[n] = l_cache + l_own

    def add(n, begin_at, count):
        top = tops[n, 0:1]
        total = sums[n]
        out = acc[n]
        for j in range(count):
            i = begin_at + j
            p, l = weigh(n, 2 + i, top)
            at = first[n] + 2 * i
            values = jnp.concatenate([v_ref[at], v_ref[at + 1]], axis=1)
            out = out + dot(values, p, ((1,), (0,)))
            total = total + l
        sums[n] = total
        acc[n] = out

    for n in BOTH:
        regions(n, add)

    for n in BOTH:
        out = acc[n] * (1.0 / jnp.sum(sums[n], axis=0, keepdims=True))
        for g in range(GROUP):
            lanes = slice(g * HD, (g + 1) * HD)
            o_refs[n][:, lanes] = out[:, lanes].astype(jnp.bfloat16).T


def attend(dx, place, docs, firsts, q0, q1, keys, values, cache):
    whole = pl.BlockSpec(memory_space=pltpu.VMEM)
    return pl.pallas_call(
        functools.partial(attend_kernel, dx),
        grid_spec=pltpu.PrefetchScalarGridSpec(
            num_scalar_prefetch=3,
            grid=(1,),
            in_specs=[whole] * 5,
            out_specs=[whole, whole],
            scratch_shapes=[
                pltpu.VMEM((2, 2 + MOST_PAIRS, PAIR, QW), jnp.float32),
                pltpu.VMEM((2, HD, QW), jnp.float32),
                pltpu.VMEM((2, 8, QW), jnp.float32),
                pltpu.VMEM((2, 8, QW), jnp.float32),
            ],
        ),
        out_shape=[jax.ShapeDtypeStruct((ROWS, QW), jnp.bfloat16)] * 2,
        cost_estimate=pl.CostEstimate(
            flops=48 * PAIR * QW * HD,
            bytes_accessed=8 * ROWS * QW,
            transcendentals=12 * PAIR * QW,
        ),
        compiler_params=pltpu.CompilerParams(vmem_limit_bytes=20 * MIB),
        name="attend",
    )(place, docs, firsts, q0, q1, keys, values, cache)


def join_kernel(places, place, *refs):
    pieces, out, sem = refs[: len(places)], refs[-2], refs[-1]
    copies = []
    for i, (dx, dl) in enumerate(places):
        head = lax.rem(place[0] + 4 - dx, 4) * 2 + lax.rem(place[2] + dl, 2)
        lanes = pl.ds(pl.multiple_of(head * QW, QW), QW)
        copies.append(pltpu.make_async_copy(pieces[i], out.at[:, lanes], sem.at[i]))
    for copy in copies:
        copy.start()
    for copy in copies:
        copy.wait()


def join(place, places, pieces, base):
    whole = pl.BlockSpec(memory_space=pltpu.VMEM)
    there = pl.BlockSpec(memory_space=pl.ANY)
    known = [] if base is None else [base]
    return pl.pallas_call(
        functools.partial(join_kernel, places),
        grid_spec=pltpu.PrefetchScalarGridSpec(
            num_scalar_prefetch=1,
            grid=(1,),
            in_specs=[whole] * len(pieces) + [there] * len(known),
            out_specs=there,
            scratch_shapes=[pltpu.SemaphoreType.DMA((len(pieces),))],
        ),
        out_shape=jax.ShapeDtypeStruct((ROWS, KVH * QW), jnp.bfloat16),
        input_output_aliases={} if base is None else {1 + len(pieces): 0},
        compiler_params=pltpu.CompilerParams(vmem_limit_bytes=4 * MIB),
        name="join",
    )(place, *pieces, *known)


def out_route(sections, dx, dl):
    route = []
    for z in range(sections):
        for x in range(4):
            for l in range(2):
                target = ((z + 1) % sections, (x + dx) % 4, l ^ dl)
                route.append(((z * 4 + x) * 2 + l, (target[0] * 4 + target[1]) * 2 + target[2]))
    return route


def query_route(dx, dl):
    return [
        (x * 2 + l, (x + 4 - dx) % 4 * 2 + (l ^ dl)) for x in range(4) for l in range(2)
    ]


def per_device(queries, keys_new, values_new, stretch_cache, hadamard_signs, stretch_docs):
    place = jnp.stack([lax.axis_index(name) for name in CTX]).astype(jnp.int32)
    sections = lax.axis_size("section")
    had = jnp.asarray(hadamard(HD), dtype=jnp.bfloat16)
    signs = hadamard_signs[0].astype(jnp.bfloat16)
    kv = pack_kv(keys_new[0], values_new[0])
    mine = lax.all_to_all(kv.reshape(N_CTX, ROWS, HD), CTX, 0, 0, tiled=True)
    q = dict(zip(offsets(), pack_q(place, queries[0])))

    def send(at):
        return lax.ppermute(q[at], ("x", "l"), query_route(*at))

    q[0, 1] = send((0, 1))
    for dx in EARLY:
        q[dx, 0], q[dx, 1] = send((dx, 0)), send((dx, 1))
    cache = turn_cache(place, stretch_cache, had)
    sign_rows = jnp.tile(signs[1], CACHE // HD)[:, None]
    pattern = jnp.stack(
        [jnp.broadcast_to(signs[0], (CACHE, HD)), jnp.broadcast_to(sign_rows, (CACHE, HD))]
    )
    mine, q, cache, pattern = lax.optimization_barrier((mine, q, cache, pattern))
    cache = cache * pattern
    other = lax.ppermute(mine, "c", [(0, 1), (1, 0)])
    for dx in LATE:
        q[dx, 0], q[dx, 1] = send((dx, 0)), send((dx, 1))
    earlier = stretch_docs[None, :] < stretch_docs[:, None]
    firsts = jnp.sum(earlier, axis=1, dtype=jnp.int32)
    keys = jnp.where(place[3] == 0, mine, other)
    values = jnp.where(place[3] == 0, other, mine)
    result = None
    for group in GROUPS:
        outs = {}
        for dx in group:
            outs[dx] = attend(
                dx, place, stretch_docs, firsts, q[dx, 0], q[dx, 1], keys, values, cache
            )
        places = [(dx, dl) for dx in reversed(group) for dl in range(2)]
        outs = lax.optimization_barrier([outs[dx][dl] for dx, dl in places])
        pieces = [
            lax.ppermute(out, ("section", "x", "l"), out_route(sections, dx, dl))
            for out, (dx, dl) in zip(outs, places)
        ]
        split = len(pieces) - 2
        if split:
            result = join(place, places[:split], pieces[:split], result)
        result = join(place, places[split:], pieces[split:], result)
    return result[None]


def solution(mesh):
    sections = mesh.shape["section"]
    split = Mesh(mesh.devices.reshape(sections, 4, 2, 2, 2), ("section",) + CTX)
    rows = P("section", CTX, None)
    in_specs = (rows, rows, rows, P("section", None, None), P("section", None, None), P())
    return jax.shard_map(
        per_device, mesh=split, in_specs=in_specs, out_specs=rows, check_vma=False
    )
```

```python
import functools

import jax
import jax.numpy as jnp
import numpy as np
from jax import lax
from jax.experimental import pallas as pl
from jax.experimental.pallas import tpu as pltpu
from jax.sharding import Mesh
from jax.sharding import PartitionSpec as P

HD = 128
ROWS = 128
KVH = 8
GROUP = 4
CACHE = 256
N_CTX = 32
DOCS = 8
QW = GROUP * HD
MIB = 1024 * 1024
EARLY = (1, 3)
LATE = (2,)
GROUPS = ((0,), (1, 3, 2))

CTX = ("x", "h", "l", "c")


def hadamard(length):
    numbers = np.arange(length)
    common = numbers[:, None] & numbers[None, :]
    parity = np.zeros((length, length), np.int64)
    for bit_place in range(max(int(length).bit_length(), 1)):
        parity = parity ^ common >> bit_place & 1
    return 1.0 - 2.0 * parity


def dot(a, b, dims):
    return lax.dot_general(a, b, (dims, ((), ())), preferred_element_type=jnp.float32)


def offsets():
    return [(dx, dl) for dx in range(4) for dl in range(2)]


def pack_q_kernel(place, q_ref, *outs):
    for (dx, dl), out in zip(offsets(), outs):
        head = lax.rem(place[0] + 4 - dx, 4) * 2 + lax.rem(place[2] + dl, 2)
        q = q_ref[:, pl.ds(pl.multiple_of(head * QW, QW), QW)]
        for g in range(GROUP):
            lanes = slice(g * HD, (g + 1) * HD)
            out[:, lanes] = q[:, lanes].T


def pack_q(place, queries):
    whole = pl.BlockSpec((ROWS, QW), lambda i, place: (0, 0))
    return pl.pallas_call(
        pack_q_kernel,
        grid_spec=pltpu.PrefetchScalarGridSpec(
            num_scalar_prefetch=1,
            grid=(1,),
            in_specs=[pl.BlockSpec((ROWS, KVH * QW), lambda i, place: (0, 0))],
            out_specs=[whole] * KVH,
        ),
        out_shape=[jax.ShapeDtypeStruct((ROWS, QW), jnp.bfloat16)] * KVH,
        cost_estimate=pl.CostEstimate(flops=0, bytes_accessed=4 * KVH * ROWS * QW, transcendentals=0),
        compiler_params=pltpu.CompilerParams(vmem_limit_bytes=60 * MIB),
        name="pack_q",
    )(place, queries)


def pack_kv_kernel(k_ref, v_ref, o_ref):
    for i in range(o_ref.shape[0]):
        for low in range(2):
            lanes = slice((2 * i + low) * HD, (2 * i + low + 1) * HD)
            keys = k_ref[:, lanes]
            values = v_ref[:, lanes].T
            for high in range(2):
                o_ref[i, high, low, 0] = keys
                o_ref[i, high, low, 1] = values


def pack_kv(keys, values):
    steps = 2
    per = 4 // steps
    return pl.pallas_call(
        pack_kv_kernel,
        grid=(steps,),
        in_specs=[pl.BlockSpec((ROWS, 2 * per * HD), lambda i: (0, i))] * 2,
        out_specs=pl.BlockSpec((per, 2, 2, 2, ROWS, HD), lambda i: (i, 0, 0, 0, 0, 0)),
        out_shape=jax.ShapeDtypeStruct((4, 2, 2, 2, ROWS, HD), jnp.bfloat16),
        cost_estimate=pl.CostEstimate(flops=0, bytes_accessed=6 * KVH * ROWS * QW // 2, transcendentals=0),
        compiler_params=pltpu.CompilerParams(vmem_limit_bytes=60 * MIB),
        name="pack_kv",
    )(keys, values)


def turn_kernel(place, ck_ref, cv_ref, had_ref, out):
    had = had_ref[...]
    for d in range(DOCS):
        rows = slice(d * CACHE, (d + 1) * CACHE)
        turned = dot(ck_ref[0, rows, :], had, ((1,), (0,))) * np.float32(HD**-0.5)
        out[d, 0] = turned.astype(jnp.bfloat16)
        turned = dot(had, cv_ref[0, rows, :], ((1,), (1,))) * np.float32(HD**-0.5)
        turned = turned.astype(jnp.bfloat16)
        for half in range(CACHE // HD):
            lanes = slice(half * HD, (half + 1) * HD)
            out[d, 1, lanes, :] = turned[:, lanes]


def turn_cache(place, cache, had):
    rows = DOCS * CACHE
    return pl.pallas_call(
        turn_kernel,
        grid_spec=pltpu.PrefetchScalarGridSpec(
            num_scalar_prefetch=1,
            grid=(1,),
            in_specs=[
                pl.BlockSpec((1, rows, HD), lambda i, at: (0, 0, at[0] * 2 + at[2])),
                pl.BlockSpec((1, rows, HD), lambda i, at: (0, 0, KVH + at[0] * 2 + at[2])),
                pl.BlockSpec((HD, HD), lambda i, at: (0, 0)),
            ],
            out_specs=pl.BlockSpec(memory_space=pltpu.VMEM),
        ),
        out_shape=jax.ShapeDtypeStruct((DOCS, 2, CACHE, HD), jnp.bfloat16),
        cost_estimate=pl.CostEstimate(
            flops=8 * DOCS * CACHE * HD * HD, bytes_accessed=8 * DOCS * CACHE * HD, transcendentals=0
        ),
        compiler_params=pltpu.CompilerParams(vmem_limit_bytes=56 * MIB),
        name="turn_cache",
    )(place, cache, cache, had)


PAIR = 2 * ROWS
MOST_PAIRS = 8
SIZES = (4, 2, 1)
BOTH = range(2)


def attend_kernel(
    dx,
    place,
    docs,
    firsts,
    q0_ref,
    q1_ref,
    k_ref,
    v_ref,
    cache_ref,
    o0_ref,
    o1_ref,
    scores,
    acc,
    tops,
    sums,
):
    q_refs, o_refs = (q0_ref, q1_ref), (o0_ref, o1_ref)
    src_x = lax.rem(place[0] + dx, 4)
    scale = np.float32(HD**-0.5 * np.log2(np.e))
    mes = [src_x * 8 + place[1] * 4 + lax.rem(place[2] + n, 2) * 2 + place[3] for n in BOTH]
    first = [firsts[me] for me in mes]
    doc = [docs[me] for me in mes]
    before = [mes[n] - first[n] for n in BOTH]
    pairs = [before[n] // 2 for n in BOTH]
    beside = [jnp.maximum(me - 1, 0) for me in mes]

    def fold(s):
        return s.reshape(-1, 8, QW)

    def regions(n, work):
        big = SIZES[0]

        def body(i, carry):
            work(n, i * big, big)
            return carry

        lax.fori_loop(0, pairs[n] // big, body, 0)
        done = pairs[n] // big * big
        for size in SIZES[1:]:
            need = (pairs[n] & size) != 0

            @pl.when(need)
            def _(done=done, size=size):
                work(n, done, size)

            done = done + jnp.where(need, size, 0)

    key_at = lax.broadcasted_iota(jnp.int32, (PAIR, QW), 0)
    query_at = lax.broadcasted_iota(jnp.int32, (PAIR, QW), 1) % ROWS + ROWS
    causal = key_at <= query_at
    for n in BOTH:
        keys = jnp.concatenate([k_ref[beside[n]], k_ref[mes[n]]], axis=0)
        lowest = jnp.where(before[n] % 2 == 1, 0, ROWS)
        s_own = dot(keys, q_refs[n][...], ((1,), (0,)))
        s_own = jnp.where(causal & (key_at >= lowest), s_own, -jnp.inf)
        scores[n, 1] = s_own
        tops[n] = jnp.max(fold(s_own), axis=0)

    def look(n, begin_at, count):
        best = tops[n]
        for j in range(count):
            i = begin_at + j
            keys = k_ref[pl.ds(first[n] + 2 * i, 2)].reshape(PAIR, HD)
            s = dot(keys, q_refs[n][...], ((1,), (0,)))
            scores[n, 2 + i] = s
            best = jnp.maximum(best, jnp.max(fold(s), axis=0))
        tops[n] = best

    for n in BOTH:
        regions(n, look)

    for n in BOTH:
        s_cache = dot(cache_ref[doc[n], 0], q_refs[n][...], ((1,), (0,)))
        scores[n, 0] = s_cache
        top = jnp.maximum(tops[n], jnp.max(fold(s_cache), axis=0))
        tops[n] = jnp.broadcast_to(jnp.max(top, axis=0, keepdims=True) * scale, (8, QW))

    def weigh(n, i, top):
        p = jnp.exp2(scores[n, i] * scale - top)
        return p.astype(jnp.bfloat16), jnp.sum(fold(p), axis=0)

    for n in BOTH:
        top = tops[n, 0:1]
        p_cache, l_cache = weigh(n, 0, top)
        p_own, l_own = weigh(n, 1, top)
        values = jnp.concatenate([v_ref[beside[n]], v_ref[mes[n]]], axis=1)
        cached = jnp.concatenate(
            [cache_ref[doc[n], 1, :HD], cache_ref[doc[n], 1, HD:]], axis=1
        )
        acc[n] = dot(cached, p_cache, ((1,), (0,))) + dot(values, p_own, ((1,), (0,)))
        sums[n] = l_cache + l_own

    def add(n, begin_at, count):
        top = tops[n, 0:1]
        total = sums[n]
        out = acc[n]
        for j in range(count):
            i = begin_at + j
            p, l = weigh(n, 2 + i, top)
            at = first[n] + 2 * i
            values = jnp.concatenate([v_ref[at], v_ref[at + 1]], axis=1)
            out = out + dot(values, p, ((1,), (0,)))
            total = total + l
        sums[n] = total
        acc[n] = out

    for n in BOTH:
        regions(n, add)

    for n in BOTH:
        out = acc[n] * (1.0 / jnp.sum(sums[n], axis=0, keepdims=True))
        for g in range(GROUP):
            lanes = slice(g * HD, (g + 1) * HD)
            o_refs[n][:, lanes] = out[:, lanes].astype(jnp.bfloat16).T


def attend(dx, place, docs, firsts, q0, q1, keys, values, cache):
    whole = pl.BlockSpec(memory_space=pltpu.VMEM)
    return pl.pallas_call(
        functools.partial(attend_kernel, dx),
        grid_spec=pltpu.PrefetchScalarGridSpec(
            num_scalar_prefetch=3,
            grid=(1,),
            in_specs=[whole] * 5,
            out_specs=[whole, whole],
            scratch_shapes=[
                pltpu.VMEM((2, 2 + MOST_PAIRS, PAIR, QW), jnp.float32),
                pltpu.VMEM((2, HD, QW), jnp.float32),
                pltpu.VMEM((2, 8, QW), jnp.float32),
                pltpu.VMEM((2, 8, QW), jnp.float32),
            ],
        ),
        out_shape=[jax.ShapeDtypeStruct((ROWS, QW), jnp.bfloat16)] * 2,
        cost_estimate=pl.CostEstimate(
            flops=48 * PAIR * QW * HD,
            bytes_accessed=8 * ROWS * QW,
            transcendentals=12 * PAIR * QW,
        ),
        compiler_params=pltpu.CompilerParams(vmem_limit_bytes=20 * MIB),
        name="attend",
    )(place, docs, firsts, q0, q1, keys, values, cache)


def join_kernel(places, place, *refs):
    pieces, out, sem = refs[: len(places)], refs[-2], refs[-1]
    copies = []
    for i, (dx, dl) in enumerate(places):
        head = lax.rem(place[0] + 4 - dx, 4) * 2 + lax.rem(place[2] + dl, 2)
        lanes = pl.ds(pl.multiple_of(head * QW, QW), QW)
        copies.append(pltpu.make_async_copy(pieces[i], out.at[:, lanes], sem.at[i]))
    for copy in copies:
        copy.start()
    for copy in copies:
        copy.wait()


def join(place, places, pieces, base):
    whole = pl.BlockSpec(memory_space=pltpu.VMEM)
    there = pl.BlockSpec(memory_space=pl.ANY)
    known = [] if base is None else [base]
    return pl.pallas_call(
        functools.partial(join_kernel, places),
        grid_spec=pltpu.PrefetchScalarGridSpec(
            num_scalar_prefetch=1,
            grid=(1,),
            in_specs=[whole] * len(pieces) + [there] * len(known),
            out_specs=there,
            scratch_shapes=[pltpu.SemaphoreType.DMA((len(pieces),))],
        ),
        out_shape=jax.ShapeDtypeStruct((ROWS, KVH * QW), jnp.bfloat16),
        input_output_aliases={} if base is None else {1 + len(pieces): 0},
        compiler_params=pltpu.CompilerParams(vmem_limit_bytes=4 * MIB),
        name="join",
    )(place, *pieces, *known)


def out_route(sections, dx, dl):
    route = []
    for z in range(sections):
        for x in range(4):
            for l in range(2):
                target = ((z + 1) % sections, (x + dx) % 4, l ^ dl)
                route.append(((z * 4 + x) * 2 + l, (target[0] * 4 + target[1]) * 2 + target[2]))
    return route


def query_route(dx, dl):
    return [
        (x * 2 + l, (x + 4 - dx) % 4 * 2 + (l ^ dl)) for x in range(4) for l in range(2)
    ]


def per_device(queries, keys_new, values_new, stretch_cache, hadamard_signs, stretch_docs):
    place = jnp.stack([lax.axis_index(name) for name in CTX]).astype(jnp.int32)
    sections = lax.axis_size("section")
    had = jnp.asarray(hadamard(HD), dtype=jnp.bfloat16)
    signs = hadamard_signs[0].astype(jnp.bfloat16)
    kv = pack_kv(keys_new[0], values_new[0])
    mine = lax.all_to_all(kv.reshape(N_CTX, ROWS, HD), CTX, 0, 0, tiled=True)
    q = dict(zip(offsets(), pack_q(place, queries[0])))

    def send(at):
        return lax.ppermute(q[at], ("x", "l"), query_route(*at))

    q[0, 1] = send((0, 1))
    for dx in EARLY:
        q[dx, 0], q[dx, 1] = send((dx, 0)), send((dx, 1))
    cache = turn_cache(place, stretch_cache, had)
    sign_rows = jnp.tile(signs[1], CACHE // HD)[:, None]
    pattern = jnp.stack(
        [jnp.broadcast_to(signs[0], (CACHE, HD)), jnp.broadcast_to(sign_rows, (CACHE, HD))]
    )
    mine, q, cache, pattern = lax.optimization_barrier((mine, q, cache, pattern))
    cache = cache * pattern
    other = lax.ppermute(mine, "c", [(0, 1), (1, 0)])
    for dx in LATE:
        q[dx, 0], q[dx, 1] = send((dx, 0)), send((dx, 1))
    earlier = stretch_docs[None, :] < stretch_docs[:, None]
    firsts = jnp.sum(earlier, axis=1, dtype=jnp.int32)
    keys = jnp.where(place[3] == 0, mine, other)
    values = jnp.where(place[3] == 0, other, mine)
    result = None
    for group in GROUPS:
        outs = {}
        for dx in group:
            outs[dx] = attend(
                dx, place, stretch_docs, firsts, q[dx, 0], q[dx, 1], keys, values, cache
            )
        places = [(dx, dl) for dx in reversed(group) for dl in range(2)]
        outs = lax.optimization_barrier([outs[dx][dl] for dx, dl in places])
        pieces = [
            lax.ppermute(out, ("section", "x", "l"), out_route(sections, dx, dl))
            for out, (dx, dl) in zip(outs, places)
        ]
        split = len(pieces) - 2
        if split:
            result = join(place, places[:split], pieces[:split], result)
        result = join(place, places[split:], pieces[split:], result)
    return result[None]


def solution(mesh):
    sections = mesh.shape["section"]
    split = Mesh(mesh.devices.reshape(sections, 4, 2, 2, 2), ("section",) + CTX)
    rows = P("section", CTX, None)
    in_specs = (rows, rows, rows, P("section", None, None), P("section", None, None), P())
    return jax.shard_map(
        per_device, mesh=split, in_specs=in_specs, out_specs=rows, check_vma=False
    )
```
